512 devices in a mesh: sub: 8 (over y, z_hi), row: 8 (over z_lo), col: 8 (over x, core).
Axes of the slice: x: 4, y: 4, z: 16 (z_hi: 2, z_lo: 8; z = z_hi * 8 + z_lo), core: 2. Of those that a mesh axis runs over, the one named last changes fastest.
Arguments:
- root_inverse: float32 [8192, 8192], P(('sub', 'row'), 'col')
- panel: float32 [8192, 2048], P(('sub', 'row'), 'col'), may hold values from -0.125 to 0.125
- pattern: int32 [64, 16], P(('sub', 'row'), 'col'), may hold values from 0 to 1, as said below
- diag_inverse: float32 [2048, 2048], P(('sub', 'row'), 'col')
Outputs:
- off_block: float32 [8192, 2048], P(('sub', 'row'), 'col')
- diag_block: float32 [2048, 2048], P(('sub', 'row'), 'col')
The draws below stay inside these ranges and needn't reach their ends.
Inputs may be any that keep to these rules, and one draw needn't show every extreme that they name: `pattern`: in every tile row, each aligned group of 2 tile columns (those of one index of col) has exactly one tile marked 1.
All inputs are finite; a program needn't handle non-finite values.
Results may differ from the reference program's by a relative error of at most 0.000078.
Values sent between devices are 32-bit elements; how exact they have to be, the bound alone decides.
A program may use at most 64 MiB of HBM per device.

```python
import math
import jax
import jax.numpy as jnp
from jax import lax

TILE = 128
TPD = 2
RT = 64
R = 8192
CT = 16
C = 2048


def draw_root_inverse(key, part):
    key = jax.random.fold_in(key, 11)
    first_key, second_key = jax.random.split(key, 2)
    raw_entries = jax.random.normal(first_key, (R, R), jnp.float32)
    symmetric = (raw_entries + raw_entries.T) * (0.7071 / math.sqrt(TPD))
    diagonal = jnp.exp(jax.random.uniform(second_key, (R,), jnp.float32, 0.0, math.log(4.0)))
    identity = jnp.eye(R, dtype=jnp.float32)
    result = symmetric + identity * diagonal[None, :]
    return result


def draw_pattern(key, part):
    key = jax.random.fold_in(key, 23)
    choices_drawn = jax.random.randint(key, (RT, CT // TPD), 0, TPD)
    slots_range = jnp.arange(TPD, dtype=jnp.int32)
    marked_tiles = (choices_drawn[:, :, None] == slots_range[None, None, :]).astype(jnp.int32)
    return marked_tiles.reshape(RT, CT)


def draw_diag_inverse(key, part):
    key = jax.random.fold_in(key, 37)
    first_key, second_key = jax.random.split(key, 2)
    raw_entries = jax.random.normal(first_key, (C, C), jnp.float32)
    symmetric = (raw_entries + raw_entries.T) * 0.5
    diagonal = jax.random.uniform(second_key, (C,), jnp.float32, 1.0, 3.0)
    identity = jnp.eye(C, dtype=jnp.float32)
    return symmetric + identity * diagonal[None, :]


def levels(stream_key, dims, cuts, low, largest):
    level = 1.0
    for dim, shards_of in cuts:
        steps = jax.random.uniform(jax.random.fold_in(jax.random.fold_in(stream_key, 6), dim), (shards_of,), jnp.float32, low / len(cuts), largest / len(cuts))
        level = level * jnp.repeat(jnp.exp(steps), dims[dim] // shards_of).reshape((-1,) + (1,) * (len(dims) - 1 - dim))
    return level


def centred(key, extent, spread, most, cuts=(), kind=jnp.bfloat16):
    gain = levels(key, extent, cuts, -0.22, 0.18) if cuts else 1.0
    entries = jax.random.normal(key, extent, jnp.float32) * spread * gain
    return jnp.minimum(jnp.maximum(entries, -most), most).astype(kind)


def setup_inputs(seed: int = 0) -> dict:
    splits = jax.random.split(jax.random.key(seed), 5)
    root_inverse = draw_root_inverse(jax.random.fold_in(splits[4], 71), 0)
    panel = centred(splits[1], (R, C), (R // (TPD * TPD)) ** -0.5, 0.125, ((0, 64), (1, 8)), jnp.float32)
    pattern = draw_pattern(jax.random.fold_in(splits[4], 71), 0)
    diag_inverse = draw_diag_inverse(jax.random.fold_in(splits[4], 71), 0)
    return {"root_inverse": root_inverse, "panel": panel, "pattern": pattern, "diag_inverse": diag_inverse}


def reference(root_inverse, panel, pattern, diag_inverse):
    tile_mask = jnp.repeat(jnp.repeat(pattern.astype(jnp.float32), TILE, axis=0), TILE, axis=1)
    masked_panel = panel * tile_mask
    product = jnp.dot(root_inverse, masked_panel, precision=lax.Precision.HIGHEST, preferred_element_type=jnp.float32)
    off_block = -(product * tile_mask)
    update = jnp.dot(masked_panel.T, off_block, precision=lax.Precision.HIGHEST, preferred_element_type=jnp.float32)
    diag_block = diag_inverse - update
    return off_block, diag_block
```

```python
import functools

import jax
import jax.numpy as jnp
from jax import lax
from jax.experimental import pallas as pl
from jax.experimental.pallas import tpu as pltpu
from jax.sharding import PartitionSpec as P

MESH = pl.DeviceIdType.MESH
T = 128
H = 136
f32, bf16 = jnp.float32, jnp.bfloat16


def device(x, y, z, k):
    return (y * 2 + z // 8, lax.rem(z, 8), x * 2 + k)


def slot_of(z):
    return lax.rem(z, 4) * 4 + z // 4


def split(v):
    hi = v.astype(bf16)
    return hi, (v - hi.astype(f32)).astype(bf16)


def dot3(ah, al, bh, bl):
    d = functools.partial(jnp.dot, preferred_element_type=f32)
    return d(ah, bh) + (d(ah, bl) + d(al, bh))


def arrived(ref, sem):
    pltpu.make_async_copy(ref, ref, sem).wait()


def kernel(
    a_ref, panel_ref, pattern_ref, diag_ref, off_ref, out_ref,
    vsend, abuf, vz, vs, vp, sy, op, ob, osend, oy,
    ahi, alo, vhi, vlo, thi, tlo, ohi, olo, ubuf, un, ured, uf,
    ss_a, rs_a, ss_vp, rs_vp, ss_sy, rs_sy, ss_far, ss_near, rs_vz, ss_sib, rs_sib,
    ss_vps, rs_vps, ss_o, rs_o, ss_oy, rs_oy, ss_un, rs_un, ss_uf, rs_uf,
):
    sub, row, col = lax.axis_index("sub"), lax.axis_index("row"), lax.axis_index("col")
    x, k = col // 2, lax.rem(col, 2)
    y, z = sub // 2, lax.rem(sub, 2) * 8 + row
    ky = y // 2
    ry = lax.rem(y, 2)
    sib = device(x, y, z, 1 - k)

    def zdev(d):
        return device(x, y, lax.rem(z + d + 16, 16), k)

    diag = jnp.logical_and(x == y, k == ky)
    bar = pltpu.get_barrier_semaphore()

    def hello(dev):
        pl.semaphore_signal(bar, inc=1, device_id=dev, device_id_type=MESH)

    hello(sib)
    for j in range(1, 4):
        for kk in range(2):
            hello(device(x, lax.rem(y + j, 4), z, kk))
    for d in (4, -4, 8, 1, -1, -2):
        hello(zdev(d))
    for r in range(2):
        for kk in range(2):
            me = jnp.logical_and(x == y, jnp.logical_and(2 * k + r == y, k == kk))

            @pl.when(jnp.logical_not(me))
            def _():
                hello(device(y, 2 * k + r, z, kk))

    p0 = pattern_ref[0, 0].astype(f32)
    p1 = pattern_ref[0, 1].astype(f32)
    vsend[0:T] = panel_ref[:, 0:T] * p0 + panel_ref[:, T:] * p1
    vsend[T:H] = jnp.zeros((8, T), f32) + p1
    pl.semaphore_wait(bar, 17 - diag.astype(jnp.int32))

    sends = []

    def send(src, dst, ss, rs, dev, start=True):
        c = pltpu.make_async_remote_copy(
            src_ref=src, dst_ref=dst, send_sem=ss, recv_sem=rs,
            device_id=dev, device_id_type=MESH,
        )
        if start:
            c.start()
        return c

    def send_or_keep(me, src, dst, ss, rs, dev):
        c = send(src, dst, ss, rs, dev, start=False)

        @pl.when(me)
        def _():
            pltpu.make_async_copy(src, dst, rs).start()

        @pl.when(jnp.logical_not(me))
        def _():
            c.start()

        sends.append((me, c))

    myslot = slot_of(z)
    for i, d in enumerate((8, 4, -4)):
        sends.append((None, send(vsend, vz.at[myslot], ss_far.at[i], rs_vz.at[myslot], zdev(d))))
    for i, d in enumerate((1, -1, 2)):
        sends.append((None, send(vsend, vz.at[myslot], ss_near.at[0, i], rs_vz.at[myslot], zdev(d))))
    sends.append((None, send(vsend, vs.at[myslot], ss_sib.at[myslot], rs_sib.at[myslot], sib)))
    for j in range(4):
        yy = lax.rem(y + j, 4)
        me = jnp.logical_and(j == 0, k == ky)
        rel = jnp.where(k == ky, 0, 1)
        i = ry * 2 + rel
        dev = device(x, yy, z, ky)
        if j == 0:
            send_or_keep(me, vsend.at[pl.ds(T, 8)], sy.at[i], ss_sy.at[j], rs_sy.at[i], dev)
        else:
            sends.append((None, send(vsend.at[pl.ds(T, 8)], sy.at[i], ss_sy.at[j], rs_sy.at[i], dev)))
    for j in (2, 1, 3, 0):
        dev = device(lax.rem(x + j, 4), x, z, ky)
        i, iv = ry * 2 + k, y * 2 + k
        if j == 0:
            send_or_keep(diag, a_ref, abuf.at[i], ss_a.at[j], rs_a.at[i], dev)
            send_or_keep(diag, vsend, vp.at[iv], ss_vp.at[j], rs_vp.at[iv], dev)
        else:
            sends.append((None, send(a_ref, abuf.at[i], ss_a.at[j], rs_a.at[i], dev)))
            sends.append((None, send(vsend, vp.at[iv], ss_vp.at[j], rs_vp.at[iv], dev)))

    def expand(ref, rel, zs):
        v, s = ref[0:T], ref[T : T + 1]
        v1 = v * s
        rows = pl.ds(pl.multiple_of(zs * T, T), T)
        for q, part in enumerate((v - v1, v1)):
            hi, lo = split(part)
            vhi[rel, rows, q * T : (q + 1) * T] = hi
            vlo[rel, rows, q * T : (q + 1) * T] = lo

    expand(vsend, 0, z)
    for i, d in enumerate((4, -4, 8)):
        zs = lax.rem(z + d + 16, 16)
        s = slot_of(zs)
        tile = vz.at[s]
        arrived(tile, rs_vz.at[s])
        for b, e in enumerate((1, -1, 2)):
            sends.append((None, send(tile, tile, ss_near.at[i + 1, b], rs_vz.at[s], zdev(e))))
        sends.append((None, send(tile, vs.at[s], ss_sib.at[s], rs_sib.at[s], sib)))
        expand(tile, 0, zs)

    for d in (-1, 1, -2):

        def near(i, carry, d=d):
            zs = lax.rem(z + d + 16 + 4 * i, 16)
            s = slot_of(zs)
            tile = vz.at[s]
            arrived(tile, rs_vz.at[s])
            send(tile, vs.at[s], ss_sib.at[s], rs_sib.at[s], sib)
            expand(tile, 0, zs)
            return carry

        lax.fori_loop(0, 4, near, 0)

    for i in range(4):
        arrived(vp.at[4 * k + i], rs_vp.at[4 * k + i])
    mine = vp.at[pl.ds(4 * k, 4)]
    sends.append((None, send(mine, mine, ss_vps, rs_vps, sib)))
    other = vp.at[pl.ds(4 * (1 - k), 4)]
    arrived(other, rs_vps)
    for ya in range(4):
        for kk in range(2):
            ref = vp.at[ya * 2 + kk]
            v, s = ref[0:T], ref[T : T + 1]
            v1 = v * s
            for q, part in enumerate((v - v1, v1)):
                hi, lo = split(part.T)
                rows = slice((kk * 2 + q) * T, (kk * 2 + q + 1) * T)
                thi[rows, ya * T : (ya + 1) * T] = hi
                tlo[rows, ya * T : (ya + 1) * T] = lo

    for r in range(2):
        for kk in range(2):
            i = r * 2 + kk
            arrived(abuf.at[i], rs_a.at[i])
            hi, lo = split(abuf[i])
            ahi[r * T : (r + 1) * T, kk * 1024 : (kk + 1) * 1024] = hi
            alo[r * T : (r + 1) * T, kk * 1024 : (kk + 1) * 1024] = lo

    def from_sibling(i, carry):
        zs = lax.rem(z + i, 16)
        s = slot_of(zs)
        arrived(vs.at[s], rs_sib.at[s])
        expand(vs.at[s], 1, zs)
        return carry

    lax.fori_loop(0, 16, from_sibling, 0)

    for r in range(2):
        for rel in range(2):
            arrived(sy.at[r * 2 + rel], rs_sy.at[r * 2 + rel])
    for rel in range(2):
        acc = dot3(ahi[...], alo[...], vhi[rel], vlo[rel])
        for r in range(2):
            i = r * 2 + rel
            s = sy[i, 0:1]
            rows = acc[r * T : (r + 1) * T]
            op[i] = jnp.where(s > 0.5, rows[:, T:], rows[:, :T])
            me = jnp.logical_and(2 * k + r == y, rel == 0)
            dev = device(x, 2 * k + r, z, k if rel == 0 else 1 - k)
            if rel == 0:
                send_or_keep(me, op.at[i], ob.at[y], ss_o.at[i], rs_o.at[y], dev)
            else:
                sends.append((None, send(op.at[i], ob.at[y], ss_o.at[i], rs_o.at[y], dev)))

    for i in range(4):
        arrived(ob.at[i], rs_o.at[i])
    o = -((ob[0] + ob[1]) + (ob[2] + ob[3]))
    osend[0:T] = o
    osend[T:H] = vsend[T:H]
    for j in range(1, 4):
        dev = device(x, lax.rem(y + j, 4), z, k)
        sends.append((None, send(osend, oy.at[y], ss_oy.at[j - 1], rs_oy.at[y], dev)))
    o1 = o * p1
    off_ref[:, 0:T] = o * p0
    off_ref[:, T:] = o1

    def place(ref, ya):
        v, s = ref[0:T], ref[T : T + 1]
        v1 = v * s
        rows = pl.ds(pl.multiple_of(ya * T, T), T)
        for q, part in enumerate((v - v1, v1)):
            hi, lo = split(part)
            ohi[rows, q * T : (q + 1) * T] = hi
            olo[rows, q * T : (q + 1) * T] = lo

    place(osend, y)
    for j in range(1, 4):
        ya = lax.rem(y + j, 4)
        arrived(oy.at[ya], rs_oy.at[ya])
        place(oy.at[ya], ya)

    for zb in range(4):
        rows = slice(zb * T, (zb + 1) * T)
        u = dot3(thi[rows], tlo[rows], ohi[...], olo[...])
        for zl in range(4):
            ubuf[zl, zb] = u[zl * 32 : (zl + 1) * 32]
    zl, zb = lax.rem(z, 4), z // 4
    for i, d in enumerate((1, -1, 2)):
        sends.append((None, send(ubuf.at[lax.rem(zl + d + 4, 4)], un.at[i], ss_un.at[i], rs_un.at[i], zdev(d))))
    for i in range(3):
        arrived(un.at[i], rs_un.at[i])
    ured[...] = (ubuf[zl] + un[0]) + (un[1] + un[2])
    for j in (2, 1, 3):
        sends.append((None, send(
            ured.at[lax.rem(zb + j, 4)], uf.at[j - 1], ss_uf.at[j - 1], rs_uf.at[j - 1], zdev(4 * j),
        )))
    total = ured[zb]
    for j in range(3):
        arrived(uf.at[j], rs_uf.at[j])
        total = total + uf[j]
    out_ref[...] = diag_ref[...] - total

    for me, c in sends:
        if me is None:
            c.wait_send()
        else:
            pl.when(jnp.logical_not(me))(c.wait_send)

    def sent(i, carry):
        for d in (-1, 1, -2):
            s = slot_of(lax.rem(z + d + 16 + 4 * i, 16))
            send(vz.at[s], vs.at[s], ss_sib.at[s], rs_sib.at[s], sib, start=False).wait_send()
        return carry

    lax.fori_loop(0, 4, sent, 0)


def local(root_inverse, panel, pattern, diag_inverse):
    vmem, dma = pltpu.VMEM, pltpu.SemaphoreType.DMA
    return pl.pallas_call(
        kernel,
        out_shape=(
            jax.ShapeDtypeStruct(panel.shape, f32),
            jax.ShapeDtypeStruct(diag_inverse.shape, f32),
        ),
        in_specs=[
            pl.BlockSpec(memory_space=pltpu.VMEM),
            pl.BlockSpec(memory_space=pltpu.VMEM),
            pl.BlockSpec(memory_space=pltpu.SMEM),
            pl.BlockSpec(memory_space=pltpu.VMEM),
        ],
        out_specs=(pl.BlockSpec(memory_space=pltpu.VMEM), pl.BlockSpec(memory_space=pltpu.VMEM)),
        scratch_shapes=[
            vmem((H, T), f32),
            vmem((4, T, 1024), f32),
            vmem((16, H, T), f32),
            vmem((16, H, T), f32),
            vmem((8, H, T), f32),
            vmem((4, 8, T), f32),
            vmem((4, T, T), f32),
            vmem((4, T, T), f32),
            vmem((H, T), f32),
            vmem((4, H, T), f32),
            vmem((2 * T, 2048), bf16),
            vmem((2 * T, 2048), bf16),
            vmem((2, 2048, 2 * T), bf16),
            vmem((2, 2048, 2 * T), bf16),
            vmem((4 * T, 4 * T), bf16),
            vmem((4 * T, 4 * T), bf16),
            vmem((4 * T, 2 * T), bf16),
            vmem((4 * T, 2 * T), bf16),
            vmem((4, 4, 32, 2 * T), f32),
            vmem((3, 4, 32, 2 * T), f32),
            vmem((4, 32, 2 * T), f32),
            vmem((3, 32, 2 * T), f32),
            dma((4,)), dma((4,)),
            dma((4,)), dma((8,)),
            dma((4,)), dma((4,)),
            dma((3,)), dma((4, 3)), dma((16,)),
            dma((16,)), dma((16,)),
            dma, dma,
            dma((4,)), dma((4,)),
            dma((3,)), dma((4,)),
            dma((3,)), dma((3,)),
            dma((3,)), dma((3,)),
        ],
        compiler_params=pltpu.CompilerParams(
            collective_id=0, has_side_effects=True, vmem_limit_bytes=48 << 20
        ),
    )(root_inverse, panel, pattern, diag_inverse)


def solution(mesh):
    spec = P(("sub", "row"), "col")
    return jax.shard_map(
        local, mesh=mesh, in_specs=(spec,) * 4, out_specs=(spec,) * 2, check_vma=False
    )
```

```python
import functools

import jax
import jax.numpy as jnp
from jax import lax
from jax.experimental import pallas as pl
from jax.experimental.pallas import tpu as pltpu
from jax.sharding import PartitionSpec as P

MESH = pl.DeviceIdType.MESH
T = 128
H = 136
f32, bf16 = jnp.float32, jnp.bfloat16


def device(x, y, z, k):
    return (y * 2 + z // 8, lax.rem(z, 8), x * 2 + k)


TREE = (
    (0, (5, -5, 1, -1)),
    (1, (2,)),
    (-1, (-2,)),
    (5, (6, 4, 8)),
    (-5, (-6, -4)),
    (2, ()),
    (-2, ()),
    (4, (3,)),
    (-4, (-3,)),
    (6, (7,)),
    (-6, (-7,)),
    (8, ()),
    (3, ()),
    (-3, ()),
    (7, ()),
    (-7, ()),
)
NEAR, FAR = (1, -1, 2), (8, 4, -4)
STEPS = sorted({c - o for o, to in TREE for c in to} | set(NEAR) | set(FAR))


def split(v):
    hi = v.astype(bf16)
    return hi, (v - hi.astype(f32)).astype(bf16)


def dot3(ah, al, bh, bl):
    d = functools.partial(jnp.dot, preferred_element_type=f32)
    return d(ah, bh) + (d(ah, bl) + d(al, bh))


def arrived(ref, sem):
    pltpu.make_async_copy(ref, ref, sem).wait()


def kernel(
    a_ref, panel_ref, pattern_ref, diag_ref, off_ref, out_ref,
    panel, diag, vsend, abuf, vz, vs, vp, vq, op, ob, osend, oy,
    ahi, alo, vhi, vlo, thi, tlo, ohi, olo, ubuf, un, ured, uf,
    ss_in, ss_a, rs_a, ss_t, rs_p, ss_p, ss_z, rs_z, ss_sib, rs_sib,
    ss_q, rs_q, ss_o, rs_o, ss_oy, rs_oy, ss_un, rs_un, ss_uf, rs_uf,
):
    sub, row, col = lax.axis_index("sub"), lax.axis_index("row"), lax.axis_index("col")
    x, k = col // 2, lax.rem(col, 2)
    y, z = sub // 2, lax.rem(sub, 2) * 8 + row
    ky = y // 2
    ry = lax.rem(y, 2)
    sib = device(x, y, z, 1 - k)

    def zat(d):
        return lax.rem(z + d + 16, 16)

    def zdev(d):
        return device(x, y, zat(d), k)

    on_diagonal = x == y
    keeps = jnp.logical_and(on_diagonal, k == ky)
    bar = pltpu.get_barrier_semaphore()

    def hello(dev):
        pl.semaphore_signal(bar, inc=1, device_id=dev, device_id_type=MESH)

    for d in STEPS:
        hello(zdev(-d))
    for j in range(1, 4):
        hello(device(lax.rem(x + j, 4), y, z, k))
        for kk in range(2):
            hello(device(x, lax.rem(y + j, 4), z, kk))
    hello(sib)

    @pl.when(jnp.logical_not(on_diagonal))
    def _():
        hello(device(y, x, z, k))

    for j in range(4):
        dev = device(lax.rem(x + j, 4), x, z, ky)
        if j == 0:
            pl.when(jnp.logical_not(keeps))(functools.partial(hello, dev))
        else:
            hello(dev)
    here = (
        pltpu.make_async_copy(panel_ref, panel, ss_in.at[0]),
        pltpu.make_async_copy(diag_ref, diag, ss_in.at[1]),
    )
    for c in here:
        c.start()
    here[0].wait()

    p0 = pattern_ref[0, 0].astype(f32)
    p1 = pattern_ref[0, 1].astype(f32)
    vsend[0:T] = panel[:, 0:T] * p0 + panel[:, T:] * p1
    vsend[T:H] = jnp.zeros((8, T), f32) + p1
    here[1].wait()
    pl.semaphore_wait(
        bar, len(STEPS) + 15 - on_diagonal.astype(jnp.int32) - keeps.astype(jnp.int32)
    )

    sends = []

    def send(src, dst, ss, rs, dev, start=True):
        c = pltpu.make_async_remote_copy(
            src_ref=src, dst_ref=dst, send_sem=ss, recv_sem=rs,
            device_id=dev, device_id_type=MESH,
        )
        if start:
            c.start()
            sends.append((None, c))
        return c

    def send_or_keep(me, src, dst, ss, rs, dev):
        c = send(src, dst, ss, rs, dev, start=False)

        @pl.when(me)
        def _():
            pltpu.make_async_copy(src, dst, rs).start()

        @pl.when(jnp.logical_not(me))
        def _():
            c.start()

        sends.append((me, c))

    def halves(ref):
        v, s = ref[0:T], ref[T : T + 1]
        v1 = v * s
        return v - v1, v1

    send_or_keep(on_diagonal, vsend, vp.at[y], ss_t, rs_p.at[y], device(y, x, z, k))
    mine = vp.at[x]
    arrived(mine, rs_p.at[x])

    def expand(ref, rel, zs):
        rows = pl.ds(pl.multiple_of(zs * T, T), T)
        for q, part in enumerate(halves(ref)):
            hi, lo = split(part)
            vhi[rel, rows, q * T : (q + 1) * T] = hi
            vlo[rel, rows, q * T : (q + 1) * T] = lo

    for n, (o, to) in enumerate(TREE):
        zs = zat(-o)
        tile = vz.at[zs] if o else mine
        if o:
            arrived(tile, rs_z.at[zs])
        for c in to:
            send(tile, vz.at[zs], ss_z.at[c + 7], rs_z.at[zs], zdev(c - o))
        send(tile, vs.at[zs], ss_sib.at[zs], rs_sib.at[zs], sib)
        if n == 0:
            for j in (2, 1, 3, 0):
                i = ry * 2 + k
                dev = device(x, lax.rem(y + j, 4), z, ky)
                if j == 0:
                    send_or_keep(k == ky, a_ref, abuf.at[i], ss_a.at[j], rs_a.at[i], dev)
                else:
                    send(a_ref, abuf.at[i], ss_a.at[j], rs_a.at[i], dev)
            for j in (2, 1, 3):
                dev = device(lax.rem(x + j, 4), y, z, k)
                send(mine, vp.at[x], ss_p.at[j - 1], rs_p.at[x], dev)
        expand(tile, 0, zs)

    for j in range(1, 4):
        i = lax.rem(x + j, 4)
        arrived(vp.at[i], rs_p.at[i])
    send(vp, vq, ss_q, rs_q, sib)
    arrived(vq, rs_q)
    for ref, kk in ((vp, k), (vq, 1 - k)):
        for ya in range(4):
            for q, part in enumerate(halves(ref.at[ya])):
                hi, lo = split(part.T)
                thi[kk * 2 + q, :, ya * T : (ya + 1) * T] = hi
                tlo[kk * 2 + q, :, ya * T : (ya + 1) * T] = lo

    for r in range(2):
        for kk in range(2):
            i = r * 2 + kk
            arrived(abuf.at[i], rs_a.at[i])
            hi, lo = split(abuf[i])
            ahi[r * T : (r + 1) * T, kk * 1024 : (kk + 1) * 1024] = hi
            alo[r * T : (r + 1) * T, kk * 1024 : (kk + 1) * 1024] = lo

    for o, _ in TREE:
        zs = zat(-o)
        arrived(vs.at[zs], rs_sib.at[zs])
        expand(vs.at[zs], 1, zs)

    for rel in range(2):
        acc = dot3(ahi[...], alo[...], vhi[rel], vlo[rel])
        for r in range(2):
            i = r * 2 + rel
            s = (vq if rel else vp)[2 * k + r, T : T + 1]
            rows = acc[r * T : (r + 1) * T]
            op[i] = jnp.where(s > 0.5, rows[:, T:], rows[:, :T])
            if rel == 0:
                me = jnp.logical_and(on_diagonal, 2 * k + r == y)
                dev = device(y, 2 * k + r, z, k)
                send_or_keep(me, op.at[i], ob.at[x], ss_o.at[i], rs_o.at[x], dev)
            else:
                dev = device(y, 2 * k + r, z, 1 - k)
                send(op.at[i], ob.at[x], ss_o.at[i], rs_o.at[x], dev)

    for i in range(4):
        arrived(ob.at[i], rs_o.at[i])
    o = -((ob[0] + ob[1]) + (ob[2] + ob[3]))
    osend[0:T] = o
    osend[T:H] = vsend[T:H]
    for j in (2, 1, 3):
        dev = device(x, lax.rem(y + j, 4), z, k)
        send(osend, oy.at[y], ss_oy.at[j - 1], rs_oy.at[y], dev)
    off_ref[:, 0:T] = o * p0
    off_ref[:, T:] = o * p1

    def place(ref, ya):
        rows = pl.ds(pl.multiple_of(ya * T, T), T)
        for q, part in enumerate(halves(ref)):
            hi, lo = split(part)
            ohi[rows, q * T : (q + 1) * T] = hi
            olo[rows, q * T : (q + 1) * T] = lo

    place(osend, y)
    for j in (1, 3, 2):
        ya = lax.rem(y + j, 4)
        arrived(oy.at[ya], rs_oy.at[ya])
        place(oy.at[ya], ya)

    zl, zb = lax.rem(z, 4), z // 4
    for j in (2, 1, 3, 0):
        b = lax.rem(zb + j, 4)
        u = dot3(thi[b], tlo[b], ohi[...], olo[...])
        for i in range(4):
            ubuf[i, b] = u[i * 32 : (i + 1) * 32]
        for i, d in enumerate(NEAR):
            src = ubuf.at[lax.rem(zl + d + 4, 4), b]
            send(src, un.at[i, b], ss_un.at[i, j], rs_un.at[i, b], zdev(d))
    for j in (2, 1, 3, 0):
        b = lax.rem(zb + j, 4)
        for i in range(3):
            arrived(un.at[i, b], rs_un.at[i, b])
        ured[b] = (ubuf[zl, b] + un[0, b]) + (un[1, b] + un[2, b])
        if j:
            send(ured.at[b], uf.at[j - 1], ss_uf.at[j - 1], rs_uf.at[j - 1], zdev(4 * j))
    total = diag[...] - ured[zb]
    for j in (0, 2, 1):
        arrived(uf.at[j], rs_uf.at[j])
        total = total - uf[j]
    out_ref[...] = total

    for me, c in sends:
        if me is None:
            c.wait_send()
        else:
            pl.when(jnp.logical_not(me))(c.wait_send)


def local(root_inverse, panel, pattern, diag_inverse):
    vmem, dma = pltpu.VMEM, pltpu.SemaphoreType.DMA
    return pl.pallas_call(
        kernel,
        out_shape=(
            jax.ShapeDtypeStruct(panel.shape, f32),
            jax.ShapeDtypeStruct(diag_inverse.shape, f32),
        ),
        in_specs=[
            pl.BlockSpec(memory_space=pl.ANY),
            pl.BlockSpec(memory_space=pl.ANY),
            pl.BlockSpec(memory_space=pltpu.SMEM),
            pl.BlockSpec(memory_space=pl.ANY),
        ],
        out_specs=(pl.BlockSpec(memory_space=pltpu.VMEM), pl.BlockSpec(memory_space=pltpu.VMEM)),
        scratch_shapes=[
            vmem((T, 2 * T), f32),
            vmem((32, 2 * T), f32),
            vmem((H, T), f32),
            vmem((4, T, 1024), f32),
            vmem((16, H, T), f32),
            vmem((16, H, T), f32),
            vmem((4, H, T), f32),
            vmem((4, H, T), f32),
            vmem((4, T, T), f32),
            vmem((4, T, T), f32),
            vmem((H, T), f32),
            vmem((4, H, T), f32),
            vmem((2 * T, 2048), bf16),
            vmem((2 * T, 2048), bf16),
            vmem((2, 2048, 2 * T), bf16),
            vmem((2, 2048, 2 * T), bf16),
            vmem((4, T, 4 * T), bf16),
            vmem((4, T, 4 * T), bf16),
            vmem((4 * T, 2 * T), bf16),
            vmem((4 * T, 2 * T), bf16),
            vmem((4, 4, 32, 2 * T), f32),
            vmem((3, 4, 32, 2 * T), f32),
            vmem((4, 32, 2 * T), f32),
            vmem((3, 32, 2 * T), f32),
            dma((2,)),
            dma((4,)), dma((4,)),
            dma, dma((4,)), dma((3,)),
            dma((16,)), dma((16,)),
            dma((16,)), dma((16,)),
            dma, dma,
            dma((4,)), dma((4,)),
            dma((3,)), dma((4,)),
            dma((3, 4)), dma((3, 4)),
            dma((3,)), dma((3,)),
        ],
        compiler_params=pltpu.CompilerParams(
            collective_id=0, has_side_effects=True, vmem_limit_bytes=56 << 20
        ),
    )(root_inverse, panel, pattern, diag_inverse)


def solution(mesh):
    spec = P(("sub", "row"), "col")
    return jax.shard_map(
        local, mesh=mesh, in_specs=(spec,) * 4, out_specs=(spec,) * 2, check_vma=False
    )
```

```python
import functools

import jax
import jax.numpy as jnp
from jax import lax
from jax.experimental import pallas as pl
from jax.experimental.pallas import tpu as pltpu
from jax.sharding import PartitionSpec as P

MESH = pl.DeviceIdType.MESH
T = 128
H = 136
f32, bf16 = jnp.float32, jnp.bfloat16


def device(x, y, z, k):
    return (y * 2 + z // 8, lax.rem(z, 8), x * 2 + k)


TREE = (
    (0, (5, -5, 1, -1)),
    (1, (2,)),
    (-1, (-2,)),
    (5, (6, 4)),
    (-5, (-6, -4)),
    (2, ()),
    (-2, ()),
    (6, (7,)),
    (-6, (-7,)),
    (4, (3,)),
    (-4, (-3,)),
    (7, (8,)),
    (-7, ()),
    (3, ()),
    (-3, ()),
    (8, ()),
)
PIECES = ((0, 64), (64, 72))
NEAR = (2, 1, -1)
STEPS = sorted({c - o for o, to in TREE for c in to} | set(NEAR))
TURNED = (8, 4, -4)


def split(v):
    hi = v.astype(bf16)
    return hi, (v - hi.astype(f32)).astype(bf16)


def dot3(ah, al, bh, bl):
    d = functools.partial(jnp.dot, preferred_element_type=f32)
    return d(ah, bh) + (d(ah, bl) + d(al, bh))


def arrived(ref, sem):
    pltpu.make_async_copy(ref, ref, sem).wait()


def kernel(
    a_ref, panel_ref, pattern_ref, diag_ref, off_ref, out_ref,
    panel, diag, abuf, vz, vs, vp, vq, sy, op, ob, osend, ohome, oy,
    ahi, alo, vhi, vlo, thi, tlo, ohi, olo, ubuf, un, ured, uf,
    ss_in, ss_a, ss_h, rs_a, ss_t, ss_p, rs_p, ss_z, rs_z, ss_sib, rs_sib, ss_sy, rs_sy,
    ss_q, rs_q, ss_o, rs_o, ss_oh, rs_oh, ss_oy, rs_oy, ss_un, rs_un, ss_uf, rs_uf,
):
    here = (
        pltpu.make_async_copy(panel_ref, panel, ss_in.at[0]),
        pltpu.make_async_copy(diag_ref, diag, ss_in.at[1]),
    )
    for c in here:
        c.start()
    sub, row, col = lax.axis_index("sub"), lax.axis_index("row"), lax.axis_index("col")
    x, k = col // 2, lax.rem(col, 2)
    y, z = sub // 2, lax.rem(sub, 2) * 8 + row
    kx, ky = x // 2, y // 2
    way = 1 - 2 * k
    sib = device(x, y, z, 1 - k)

    def zat(d):
        return lax.rem(z + way * d + 16, 16)

    def zdev(d):
        return device(x, y, zat(d), k)

    def turned(d):
        return device(y, x, zat(d), k)

    on_diagonal = x == y
    bar = pltpu.get_barrier_semaphore()

    def hello(dev):
        pl.semaphore_signal(bar, inc=1, device_id=dev, device_id_type=MESH)

    for d in STEPS:
        hello(zdev(-d))
    for j in range(1, 4):
        for kk in range(2):
            hello(device(lax.rem(x + j, 4), y, z, kk))
            hello(device(x, lax.rem(y + j, 4), z, kk))
    hello(sib)

    @pl.when(jnp.logical_not(on_diagonal))
    def _():
        hello(turned(0))

    here[0].wait()

    p0 = pattern_ref[0, 0].astype(f32)
    p1 = pattern_ref[0, 1].astype(f32)
    vp[y, 0:T] = panel[:, 0:T] * p0 + panel[:, T:] * p1
    vp[y, T:H] = jnp.zeros((8, T), f32) + p1
    pl.semaphore_wait(bar, len(STEPS) + 14 - on_diagonal.astype(jnp.int32))

    sends = []

    def send(src, dst, ss, rs, dev, start=True):
        c = pltpu.make_async_remote_copy(
            src_ref=src, dst_ref=dst, send_sem=ss, recv_sem=rs,
            device_id=dev, device_id_type=MESH,
        )
        if start:
            c.start()
            sends.append((None, c))
        return c

    def send_or_keep(me, src, dst, ss, rs, dev):
        c = send(src, dst, ss, rs, dev, start=False)

        @pl.when(me)
        def _():
            pltpu.make_async_copy(src, dst, rs).start()

        @pl.when(jnp.logical_not(me))
        def _():
            c.start()

        sends.append((me, c))

    def halves(ref):
        v, s = ref[0:T], ref[T : T + 1]
        v1 = v * s
        return v - v1, v1

    v = vp.at[y]
    for n, piece in enumerate(PIECES):
        ds = pl.ds(*piece)
        send_or_keep(
            on_diagonal, vp.at[y, ds], vz.at[z, ds], ss_t.at[n], rs_z.at[n, z], turned(0)
        )
    for j in (2, 1, 3):
        send(v, v, ss_p.at[j - 1], rs_p.at[y], device(x, lax.rem(y + j, 4), z, k))

    def half(i, h):
        return abuf.at[i, pl.ds(h * 64, 64)]

    def send_a():
        i = lax.rem(y, 2) * 2 + k
        for h in (0, 1):
            for j, h in ((1, h), (3, 1 - h), (0, h)):
                src = a_ref.at[pl.ds(h * 64, 64)]
                dev = device(x, lax.rem(y + j, 4), z, ky)
                if j == 0:
                    send_or_keep(k == ky, src, half(i, h), ss_a.at[j, h], rs_a.at[i, h], dev)
                else:
                    send(src, half(i, h), ss_a.at[j, h], rs_a.at[i, h], dev)

    def hand_on_a():
        for r in range(2):
            d = lax.rem(y - 2 * k - r + 4, 4)
            h = jnp.where(d == 1, 0, 1)
            dev = device(x, jnp.where(d == 1, lax.rem(y + 1, 4), lax.rem(y + 3, 4)), z, k)
            for kk in range(2):
                i = r * 2 + kk
                c = send(half(i, h), half(i, h), ss_h.at[i], rs_a.at[i, h], dev, start=False)

                @pl.when(lax.rem(d, 2) == 1)
                def _():
                    arrived(half(i, h), rs_a.at[i, h])
                    c.start()

                sends.append((lax.rem(d, 2) == 0, c))

    def expand(ref, rel, zs):
        rows = pl.ds(pl.multiple_of(zs * T, T), T)
        for q, part in enumerate(halves(ref)):
            hi, lo = split(part)
            vhi[rel, rows, q * T : (q + 1) * T] = hi
            vlo[rel, rows, q * T : (q + 1) * T] = lo

    for o, to in TREE:
        zs = zat(-o)
        tile = vz.at[zs]
        for n, piece in enumerate(PIECES):
            part = vz.at[zs, pl.ds(*piece)]
            arrived(part, rs_z.at[n, zs])
            for c in to:
                send(part, part, ss_z.at[n, c + 7], rs_z.at[n, zs], zdev(c - o))
        send(tile, vs.at[zs], ss_sib.at[zs], rs_sib.at[zs], sib)
        if o == -5:
            hand_on_a()
        if o == 0:
            send_a()
            for j in (2, 1, 3, 0):
                i = lax.rem(x, 2) * 2 + jnp.where(k == kx, 0, 1)
                dev = device(lax.rem(x + j, 4), y, z, kx)
                src = vz.at[z, pl.ds(T, 8)]
                if j == 0:
                    send_or_keep(k == kx, src, sy.at[i], ss_sy.at[j], rs_sy.at[i], dev)
                else:
                    send(src, sy.at[i], ss_sy.at[j], rs_sy.at[i], dev)
        expand(tile, 0, zs)

    for j in range(1, 4):
        i = lax.rem(y + j, 4)
        arrived(vp.at[i], rs_p.at[i])
    send(vp, vq, ss_q, rs_q, sib)
    arrived(vq, rs_q)
    for ref, kk in ((vp, k), (vq, 1 - k)):
        for ya in range(4):
            for q, part in enumerate(halves(ref.at[ya])):
                hi, lo = split(part.T)
                thi[kk * 2 + q, :, ya * T : (ya + 1) * T] = hi
                tlo[kk * 2 + q, :, ya * T : (ya + 1) * T] = lo

    for r in range(2):
        for kk in range(2):
            i = r * 2 + kk
            d = lax.rem(y - 2 * k - r + 4, 4)
            h = jnp.where(d == 1, 0, 1)

            @pl.when(lax.rem(d, 2) == 0)
            def _():
                arrived(half(i, h), rs_a.at[i, h])

            arrived(half(i, 1 - h), rs_a.at[i, 1 - h])
            hi, lo = split(abuf[i])
            ahi[r * T : (r + 1) * T, kk * 1024 : (kk + 1) * 1024] = hi
            alo[r * T : (r + 1) * T, kk * 1024 : (kk + 1) * 1024] = lo

    for o, _ in TREE:
        zs = zat(-o)
        arrived(vs.at[zs], rs_sib.at[zs])
        expand(vs.at[zs], 1, zs)
    for i in range(4):
        arrived(sy.at[i], rs_sy.at[i])

    for rel in range(2):
        acc = dot3(ahi[...], alo[...], vhi[rel], vlo[rel])
        for r in range(2):
            i = r * 2 + rel
            s = sy[i, 0:1]
            rows = acc[r * T : (r + 1) * T]
            op[i] = jnp.where(s > 0.5, rows[:, T:], rows[:, :T])
    for h in range(2):
        ds = pl.ds(h * 64, 64)
        for rel in range(2):
            for r in range(2):
                i = r * 2 + rel
                src, dst = op.at[i, ds], ob.at[x, ds]
                sems = ss_o.at[h, i], rs_o.at[h, x]
                if rel == 0:
                    send_or_keep(2 * k + r == x, src, dst, *sems, device(2 * k + r, y, z, k))
                else:
                    send(src, dst, *sems, device(2 * k + r, y, z, 1 - k))
    osend[T:H] = vz[z, T:H]
    for h, piece in enumerate(PIECES):
        lo = slice(h * 64, h * 64 + 64)
        for i in range(4):
            arrived(ob.at[i, pl.ds(h * 64, 64)], rs_o.at[h, i])
        osend[lo] = -((ob[0, lo] + ob[1, lo]) + (ob[2, lo] + ob[3, lo]))
        for j in (2, 1, 3):
            dev = device(lax.rem(x + j, 4), y, z, k)
            ds = pl.ds(*piece)
            send(osend.at[ds], oy.at[x, ds], ss_oy.at[h, j - 1], rs_oy.at[h, x], dev)
    send_or_keep(on_diagonal, osend.at[pl.ds(0, T)], ohome, ss_oh, rs_oh, turned(0))

    def place(ref, ya):
        rows = pl.ds(pl.multiple_of(ya * T, T), T)
        for q, part in enumerate(halves(ref)):
            hi, lo = split(part)
            ohi[rows, q * T : (q + 1) * T] = hi
            olo[rows, q * T : (q + 1) * T] = lo

    place(osend, x)
    for j in (1, 3, 2):
        xa = lax.rem(x + j, 4)
        for h, piece in enumerate(PIECES):
            arrived(oy.at[xa, pl.ds(*piece)], rs_oy.at[h, xa])
        place(oy.at[xa], xa)

    zl, zb = lax.rem(z, 4), z // 4
    for j in (2, 1, 3, 0):
        b = lax.rem(zb + j, 4)
        u = dot3(thi[b], tlo[b], ohi[...], olo[...])
        for i in range(4):
            ubuf[i, b] = u[i * 32 : (i + 1) * 32]
        for i, d in enumerate(NEAR):
            src = ubuf.at[lax.rem(zl + way * d + 4, 4), b]
            send(src, un.at[i, b], ss_un.at[i, j], rs_un.at[i, b], zdev(d))
    arrived(ohome, rs_oh)
    off_ref[:, 0:T] = ohome[...] * p0
    off_ref[:, T:] = ohome[...] * p1
    for j in (2, 1, 3, 0):
        b = lax.rem(zb + j, 4)
        for i in range(3):
            arrived(un.at[i, b], rs_un.at[i, b])
        ured[b] = (ubuf[zl, b] + un[0, b]) + (un[1, b] + un[2, b])
        dev = device(y, x, lax.rem(z + 4 * j, 16), k)
        if j:
            send(ured.at[b], uf.at[j], ss_uf.at[j], rs_uf.at[j], dev)
        else:
            send_or_keep(on_diagonal, ured.at[b], uf.at[j], ss_uf.at[j], rs_uf.at[j], dev)
    here[1].wait()
    total = diag[...]
    for j in (0, 1, 3, 2):
        arrived(uf.at[j], rs_uf.at[j])
        total = total - uf[j]
    out_ref[...] = total

    for me, c in sends:
        if me is None:
            c.wait_send()
        else:
            pl.when(jnp.logical_not(me))(c.wait_send)


def local(root_inverse, panel, pattern, diag_inverse):
    vmem, dma = pltpu.VMEM, pltpu.SemaphoreType.DMA
    return pl.pallas_call(
        kernel,
        out_shape=(
            jax.ShapeDtypeStruct(panel.shape, f32),
            jax.ShapeDtypeStruct(diag_inverse.shape, f32),
        ),
        in_specs=[
            pl.BlockSpec(memory_space=pl.ANY),
            pl.BlockSpec(memory_space=pl.ANY),
            pl.BlockSpec(memory_space=pltpu.SMEM),
            pl.BlockSpec(memory_space=pl.ANY),
        ],
        out_specs=(pl.BlockSpec(memory_space=pltpu.VMEM), pl.BlockSpec(memory_space=pltpu.VMEM)),
        scratch_shapes=[
            vmem((T, 2 * T), f32),
            vmem((32, 2 * T), f32),
            vmem((4, T, 1024), f32),
            vmem((16, H, T), f32),
            vmem((16, H, T), f32),
            vmem((4, H, T), f32),
            vmem((4, H, T), f32),
            vmem((4, 8, T), f32),
            vmem((4, T, T), f32),
            vmem((4, T, T), f32),
            vmem((H, T), f32),
            vmem((T, T), f32),
            vmem((4, H, T), f32),
            vmem((2 * T, 2048), bf16),
            vmem((2 * T, 2048), bf16),
            vmem((2, 2048, 2 * T), bf16),
            vmem((2, 2048, 2 * T), bf16),
            vmem((4, T, 4 * T), bf16),
            vmem((4, T, 4 * T), bf16),
            vmem((4 * T, 2 * T), bf16),
            vmem((4 * T, 2 * T), bf16),
            vmem((4, 4, 32, 2 * T), f32),
            vmem((3, 4, 32, 2 * T), f32),
            vmem((4, 32, 2 * T), f32),
            vmem((4, 32, 2 * T), f32),
            dma((2,)),
            dma((4, 2)), dma((4,)), dma((4, 2)),
            dma((2,)), dma((3,)), dma((4,)),
            dma((2, 16)), dma((2, 16)),
            dma((16,)), dma((16,)),
            dma((4,)), dma((4,)),
            dma, dma,
            dma((2, 4)), dma((2, 4)),
            dma, dma,
            dma((2, 3)), dma((2, 4)),
            dma((3, 4)), dma((3, 4)),
            dma((4,)), dma((4,)),
        ],
        compiler_params=pltpu.CompilerParams(
            collective_id=0, has_side_effects=True, vmem_limit_bytes=56 << 20
        ),
    )(root_inverse, panel, pattern, diag_inverse)


def solution(mesh):
    spec = P(("sub", "row"), "col")
    return jax.shard_map(
        local, mesh=mesh, in_specs=(spec,) * 4, out_specs=(spec,) * 2, check_vma=False
    )
```

```python
import functools

import jax
import jax.numpy as jnp
from jax import lax
from jax.experimental import pallas as pl
from jax.experimental.pallas import tpu as pltpu
from jax.sharding import PartitionSpec as P

MESH = pl.DeviceIdType.MESH
T = 128
H = 136
f32, bf16 = jnp.float32, jnp.bfloat16


def device(x, y, z, k):
    return (y * 2 + z // 8, lax.rem(z, 8), x * 2 + k)


TREE = (
    (0, (5, -5, 1, -1)),
    (1, (2,)),
    (-1, (-2,)),
    (5, (6, 4)),
    (-5, (-6, -4)),
    (2, ()),
    (-2, ()),
    (6, (7,)),
    (-6, (-7,)),
    (4, (3,)),
    (-4, (-3,)),
    (7, (8,)),
    (-7, ()),
    (3, ()),
    (-3, ()),
    (8, ()),
)
PIECES = ((0, 64), (64, 72))
NEAR = (2, 1, -1)
STEPS = sorted({c - o for o, to in TREE for c in to})
TURNED = (8, 4, -4)


def split(v):
    hi = v.astype(bf16)
    return hi, (v - hi.astype(f32)).astype(bf16)


def dot3(ah, al, bh, bl):
    d = functools.partial(jnp.dot, preferred_element_type=f32)
    return d(ah, bh) + (d(ah, bl) + d(al, bh))


def arrived(ref, sem):
    pltpu.make_async_copy(ref, ref, sem).wait()


def kernel(
    a_ref, panel_ref, pattern_ref, diag_ref, off_ref, out_ref,
    panel, diag, abuf, vz, vs, vp, vq, sy, op, ob, osend, ohome, oy,
    ahi, alo, vhi, vlo, thi, tlo, ohi, olo, ubuf, un, ured, uf,
    ss_in, ss_a, ss_h, rs_a, ss_t, ss_p, rs_p, ss_z, rs_z, ss_sib, rs_sib, ss_sy, rs_sy,
    ss_q, rs_q, ss_o, rs_o, ss_oh, rs_oh, ss_oy, rs_oy, ss_un, rs_un, ss_uf, rs_uf,
):
    here = (
        pltpu.make_async_copy(panel_ref, panel, ss_in.at[0]),
        pltpu.make_async_copy(diag_ref, diag, ss_in.at[1]),
    )
    for c in here:
        c.start()
    sub, row, col = lax.axis_index("sub"), lax.axis_index("row"), lax.axis_index("col")
    x, k = col // 2, lax.rem(col, 2)
    y, z = sub // 2, lax.rem(sub, 2) * 8 + row
    kx, ky = x // 2, y // 2
    way = 1 - 2 * k
    sib = device(x, y, z, 1 - k)

    def zat(d):
        return lax.rem(z + way * d + 16, 16)

    def zdev(d):
        return device(x, y, zat(d), k)

    def turned(d):
        return device(y, x, zat(d), k)

    on_diagonal = x == y
    bar = pltpu.get_barrier_semaphore()

    def hello(dev):
        pl.semaphore_signal(bar, inc=1, device_id=dev, device_id_type=MESH)

    for d in STEPS:
        hello(zdev(-d))
    for j in range(1, 4):
        for kk in range(2):
            hello(device(lax.rem(x + j, 4), y, z, kk))
            hello(device(x, lax.rem(y + j, 4), z, kk))
    hello(sib)

    @pl.when(jnp.logical_not(on_diagonal))
    def _():
        hello(turned(0))

    here[0].wait()

    p0 = pattern_ref[0, 0].astype(f32)
    p1 = pattern_ref[0, 1].astype(f32)
    vp[y, 0:T] = panel[:, 0:T] * p0 + panel[:, T:] * p1
    vp[y, T:H] = jnp.zeros((8, T), f32) + p1
    pl.semaphore_wait(bar, len(STEPS) + 14 - on_diagonal.astype(jnp.int32))

    sends = []

    def send(src, dst, ss, rs, dev, start=True):
        c = pltpu.make_async_remote_copy(
            src_ref=src, dst_ref=dst, send_sem=ss, recv_sem=rs,
            device_id=dev, device_id_type=MESH,
        )
        if start:
            c.start()
            sends.append((None, c))
        return c

    def drain():
        for me, c in sends:
            if me is None:
                c.wait_send()
            else:
                pl.when(jnp.logical_not(me))(c.wait_send)
        sends.clear()

    def send_or_keep(me, src, dst, ss, rs, dev):
        c = send(src, dst, ss, rs, dev, start=False)

        @pl.when(me)
        def _():
            pltpu.make_async_copy(src, dst, rs).start()

        @pl.when(jnp.logical_not(me))
        def _():
            c.start()

        sends.append((me, c))

    def halves(ref):
        v, s = ref[0:T], ref[T : T + 1]
        v1 = v * s
        return v - v1, v1

    v = vp.at[y]
    for n, piece in enumerate(PIECES):
        ds = pl.ds(*piece)
        send_or_keep(
            on_diagonal, vp.at[y, ds], vz.at[z, ds], ss_t.at[n], rs_z.at[n, z], turned(0)
        )
    for j in (2, 1, 3):
        send(v, v, ss_p.at[j - 1], rs_p.at[y], device(x, lax.rem(y + j, 4), z, k))

    def half(i, h):
        return abuf.at[i, pl.ds(h * 64, 64)]

    def send_a():
        i = lax.rem(y, 2) * 2 + k
        for h in (0, 1):
            for j, h in ((1, h), (3, 1 - h), (0, h)):
                src = a_ref.at[pl.ds(h * 64, 64)]
                dev = device(x, lax.rem(y + j, 4), z, ky)
                if j == 0:
                    send_or_keep(k == ky, src, half(i, h), ss_a.at[j, h], rs_a.at[i, h], dev)
                else:
                    send(src, half(i, h), ss_a.at[j, h], rs_a.at[i, h], dev)

    def hand_on_a():
        for r in range(2):
            d = lax.rem(y - 2 * k - r + 4, 4)
            h = jnp.where(d == 1, 0, 1)
            dev = device(x, jnp.where(d == 1, lax.rem(y + 1, 4), lax.rem(y + 3, 4)), z, k)
            for kk in range(2):
                i = r * 2 + kk
                c = send(half(i, h), half(i, h), ss_h.at[i], rs_a.at[i, h], dev, start=False)

                @pl.when(lax.rem(d, 2) == 1)
                def _():
                    arrived(half(i, h), rs_a.at[i, h])
                    c.start()

                sends.append((lax.rem(d, 2) == 0, c))

    def expand(ref, rel, zs):
        rows = pl.ds(pl.multiple_of(zs * T, T), T)
        for q, part in enumerate(halves(ref)):
            hi, lo = split(part)
            vhi[rel, rows, q * T : (q + 1) * T] = hi
            vlo[rel, rows, q * T : (q + 1) * T] = lo

    for o, to in TREE:
        zs = zat(-o)
        tile = vz.at[zs]
        for n, piece in enumerate(PIECES):
            part = vz.at[zs, pl.ds(*piece)]
            arrived(part, rs_z.at[n, zs])
            for c in to:
                send(part, part, ss_z.at[n, c + 7], rs_z.at[n, zs], zdev(c - o))
        send(tile, vs.at[zs], ss_sib.at[zs], rs_sib.at[zs], sib)
        if o == -5:
            hand_on_a()
        if o == 0:
            send_a()
            for j in (2, 1, 3, 0):
                i = lax.rem(x, 2) * 2 + jnp.where(k == kx, 0, 1)
                dev = device(lax.rem(x + j, 4), y, z, kx)
                src = vz.at[z, pl.ds(T, 8)]
                if j == 0:
                    send_or_keep(k == kx, src, sy.at[i], ss_sy.at[j], rs_sy.at[i], dev)
                else:
                    send(src, sy.at[i], ss_sy.at[j], rs_sy.at[i], dev)
        expand(tile, 0, zs)

    for j in range(1, 4):
        i = lax.rem(y + j, 4)
        arrived(vp.at[i], rs_p.at[i])
    send(vp, vq, ss_q, rs_q, sib)
    arrived(vq, rs_q)
    for ref, kk in ((vp, k), (vq, 1 - k)):
        for ya in range(4):
            for q, part in enumerate(halves(ref.at[ya])):
                hi, lo = split(part.T)
                thi[kk * 2 + q, :, ya * T : (ya + 1) * T] = hi
                tlo[kk * 2 + q, :, ya * T : (ya + 1) * T] = lo

    for r in range(2):
        for kk in range(2):
            i = r * 2 + kk
            d = lax.rem(y - 2 * k - r + 4, 4)
            h = jnp.where(d == 1, 0, 1)

            @pl.when(lax.rem(d, 2) == 0)
            def _():
                arrived(half(i, h), rs_a.at[i, h])

            arrived(half(i, 1 - h), rs_a.at[i, 1 - h])
            hi, lo = split(abuf[i])
            ahi[r * T : (r + 1) * T, kk * 1024 : (kk + 1) * 1024] = hi
            alo[r * T : (r + 1) * T, kk * 1024 : (kk + 1) * 1024] = lo

    for o, _ in TREE:
        zs = zat(-o)
        arrived(vs.at[zs], rs_sib.at[zs])
        expand(vs.at[zs], 1, zs)
    for i in range(4):
        arrived(sy.at[i], rs_sy.at[i])

    for rel in range(2):
        acc = dot3(ahi[...], alo[...], vhi[rel], vlo[rel])
        for r in range(2):
            i = r * 2 + rel
            s = sy[i, 0:1]
            rows = acc[r * T : (r + 1) * T]
            op[i] = jnp.where(s > 0.5, rows[:, T:], rows[:, :T])
        for h in range(2):
            ds = pl.ds(h * 64, 64)
            for r in range(2):
                i = r * 2 + rel
                src, dst = op.at[i, ds], ob.at[x, ds]
                sems = ss_o.at[h, i], rs_o.at[h, x]
                if rel == 0:
                    send_or_keep(2 * k + r == x, src, dst, *sems, device(2 * k + r, y, z, k))
                else:
                    send(src, dst, *sems, device(2 * k + r, y, z, 1 - k))
    osend[T:H] = vz[z, T:H]
    for h, piece in enumerate(PIECES):
        lo = slice(h * 64, h * 64 + 64)
        for i in range(4):
            arrived(ob.at[i, pl.ds(h * 64, 64)], rs_o.at[h, i])
        osend[lo] = -((ob[0, lo] + ob[1, lo]) + (ob[2, lo] + ob[3, lo]))
        for j in (2, 1, 3):
            dev = device(lax.rem(x + j, 4), y, z, k)
            ds = pl.ds(*piece)
            send(osend.at[ds], oy.at[x, ds], ss_oy.at[h, j - 1], rs_oy.at[h, x], dev)
    send_or_keep(on_diagonal, osend.at[pl.ds(0, T)], ohome, ss_oh, rs_oh, turned(0))

    drain()

    def place(ref, ya):
        rows = pl.ds(pl.multiple_of(ya * T, T), T)
        for q, part in enumerate(halves(ref)):
            hi, lo = split(part)
            ohi[rows, q * T : (q + 1) * T] = hi
            olo[rows, q * T : (q + 1) * T] = lo

    place(osend, x)
    for j in (1, 3, 2):
        xa = lax.rem(x + j, 4)
        for h, piece in enumerate(PIECES):
            arrived(oy.at[xa, pl.ds(*piece)], rs_oy.at[h, xa])
        place(oy.at[xa], xa)

    zl, zb = lax.rem(z, 4), z // 4
    for j in (2, 1, 3, 0):
        b = lax.rem(zb + j, 4)
        u = dot3(thi[b], tlo[b], ohi[...], olo[...])
        for i in range(4):
            ubuf[i, b] = u[i * 32 : (i + 1) * 32]
        for i, d in enumerate(NEAR):
            src = ubuf.at[lax.rem(zl + way * d + 4, 4), b]
            send(src, un.at[i, b], ss_un.at[i, j], rs_un.at[i, b], zdev(d))
    drain()
    arrived(ohome, rs_oh)
    off_ref[...] = ohome[...]
    for j in (2, 1, 3, 0):
        b = lax.rem(zb + j, 4)
        for i in range(3):
            arrived(un.at[i, b], rs_un.at[i, b])
        ured[b] = (ubuf[zl, b] + un[0, b]) + (un[1, b] + un[2, b])
        dev = device(y, x, lax.rem(z + 4 * j, 16), k)
        if j:
            send(ured.at[b], uf.at[j], ss_uf.at[j], rs_uf.at[j], dev)
        else:
            send_or_keep(on_diagonal, ured.at[b], uf.at[j], ss_uf.at[j], rs_uf.at[j], dev)
    here[1].wait()
    total = diag[...]
    for j in (0, 1, 3, 2):
        arrived(uf.at[j], rs_uf.at[j])
        total = total - uf[j]
    out_ref[...] = total

    drain()


def place_results(o_ref, diag_ref, pattern_ref, off_out, diag_out):
    off_out[:, 0:T] = o_ref[...] * pattern_ref[0, 0].astype(f32)
    off_out[:, T:] = o_ref[...] * pattern_ref[0, 1].astype(f32)
    diag_out[...] = diag_ref[...]


def local(root_inverse, panel, pattern, diag_inverse):
    vmem, dma = pltpu.VMEM, pltpu.SemaphoreType.DMA
    parts = pl.pallas_call(
        kernel,
        out_shape=(
            jax.ShapeDtypeStruct((T, T), f32),
            jax.ShapeDtypeStruct(diag_inverse.shape, f32),
        ),
        in_specs=[
            pl.BlockSpec(memory_space=pl.ANY),
            pl.BlockSpec(memory_space=pl.ANY),
            pl.BlockSpec(memory_space=pltpu.SMEM),
            pl.BlockSpec(memory_space=pl.ANY),
        ],
        out_specs=(pl.BlockSpec(memory_space=pltpu.VMEM), pl.BlockSpec(memory_space=pltpu.VMEM)),
        scratch_shapes=[
            vmem((T, 2 * T), f32),
            vmem((32, 2 * T), f32),
            vmem((4, T, 1024), f32),
            vmem((16, H, T), f32),
            vmem((16, H, T), f32),
            vmem((4, H, T), f32),
            vmem((4, H, T), f32),
            vmem((4, 8, T), f32),
            vmem((4, T, T), f32),
            vmem((4, T, T), f32),
            vmem((H, T), f32),
            vmem((T, T), f32),
            vmem((4, H, T), f32),
            vmem((2 * T, 2048), bf16),
            vmem((2 * T, 2048), bf16),
            vmem((2, 2048, 2 * T), bf16),
            vmem((2, 2048, 2 * T), bf16),
            vmem((4, T, 4 * T), bf16),
            vmem((4, T, 4 * T), bf16),
            vmem((4 * T, 2 * T), bf16),
            vmem((4 * T, 2 * T), bf16),
            vmem((4, 4, 32, 2 * T), f32),
            vmem((3, 4, 32, 2 * T), f32),
            vmem((4, 32, 2 * T), f32),
            vmem((4, 32, 2 * T), f32),
            dma((2,)),
            dma((4, 2)), dma((4,)), dma((4, 2)),
            dma((2,)), dma((3,)), dma((4,)),
            dma((2, 16)), dma((2, 16)),
            dma((16,)), dma((16,)),
            dma((4,)), dma((4,)),
            dma, dma,
            dma((2, 4)), dma((2, 4)),
            dma, dma,
            dma((2, 3)), dma((2, 4)),
            dma((3, 4)), dma((3, 4)),
            dma((4,)), dma((4,)),
        ],
        compiler_params=pltpu.CompilerParams(
            collective_id=0, has_side_effects=True, vmem_limit_bytes=56 << 20
        ),
    )(root_inverse, panel, pattern, diag_inverse)
    return pl.pallas_call(
        place_results,
        out_shape=tuple(jax.ShapeDtypeStruct(p.shape, f32) for p in (panel, diag_inverse)),
        in_specs=[
            pl.BlockSpec(memory_space=pltpu.VMEM),
            pl.BlockSpec(memory_space=pltpu.VMEM),
            pl.BlockSpec(memory_space=pltpu.SMEM),
        ],
        out_specs=(pl.BlockSpec(memory_space=pltpu.VMEM), pl.BlockSpec(memory_space=pltpu.VMEM)),
    )(*parts, pattern)


def solution(mesh):
    spec = P(("sub", "row"), "col")
    return jax.shard_map(
        local, mesh=mesh, in_specs=(spec,) * 4, out_specs=(spec,) * 2, check_vma=False
    )
```

```python
import functools

import jax
import jax.numpy as jnp
from jax import lax
from jax.experimental import pallas as pl
from jax.experimental.pallas import tpu as pltpu
from jax.sharding import PartitionSpec as P

MESH = pl.DeviceIdType.MESH
T = 128
H = 136
f32, bf16 = jnp.float32, jnp.bfloat16


def device(x, y, z, k):
    return (y * 2 + z // 8, lax.rem(z, 8), x * 2 + k)


TREE = (
    (0, (5, -5, 1, -1)),
    (1, (2,)),
    (-1, (-2,)),
    (5, (6, 4)),
    (-5, (-6, -4)),
    (2, ()),
    (-2, ()),
    (6, (7,)),
    (-6, (-7,)),
    (4, (3,)),
    (-4, (-3,)),
    (7, (8,)),
    (-7, ()),
    (3, ()),
    (-3, ()),
    (8, ()),
)
GROUPS = ((0, 1), (1, 3), (3, 5), (5, 7), (7, 11), (11, 15), (15, 16))
PIECES = ((0, 64), (64, 72))
NEAR = (2, 1, -1)
STEPS = sorted({c - o for o, to in TREE for c in to})
TURNED = (8, 4, -4)


def split(v):
    hi = v.astype(bf16)
    return hi, (v - hi.astype(f32)).astype(bf16)


def dot3(ah, al, bh, bl):
    d = functools.partial(jnp.dot, preferred_element_type=f32)
    return d(ah, bh) + (d(ah, bl) + d(al, bh))


def arrived(ref, sem):
    pltpu.make_async_copy(ref, ref, sem).wait()


def kernel(
    a_ref, panel_ref, pattern_ref, diag_ref, off_ref, out_ref,
    panel, diag, abuf, vz, vs, vp, vq, sy, op, ob, osend, ohome, oy,
    ahi, alo, vhi, vlo, thi, tlo, ohi, olo, ubuf, un, ured, uf,
    ss_in, ss_a, ss_h, rs_a, ss_t, ss_p, rs_p, ss_z, rs_z, ss_sib, rs_sib, ss_sy, rs_sy,
    ss_q, rs_q, ss_o, rs_o, ss_oh, rs_oh, ss_oy, rs_oy, ss_un, rs_un, ss_uf, rs_uf,
):
    here = (
        pltpu.make_async_copy(panel_ref, panel, ss_in.at[0]),
        pltpu.make_async_copy(diag_ref, diag, ss_in.at[1]),
    )
    for c in here:
        c.start()
    sub, row, col = lax.axis_index("sub"), lax.axis_index("row"), lax.axis_index("col")
    x, k = col // 2, lax.rem(col, 2)
    y, z = sub // 2, lax.rem(sub, 2) * 8 + row
    kx, ky = x // 2, y // 2
    way = 1 - 2 * k
    sib = device(x, y, z, 1 - k)

    def zat(d):
        return lax.rem(z + way * d + 16, 16)

    def zdev(d):
        return device(x, y, zat(d), k)

    def turned(d):
        return device(y, x, zat(d), k)

    on_diagonal = x == y
    bar = pltpu.get_barrier_semaphore()

    def hello(dev):
        pl.semaphore_signal(bar, inc=1, device_id=dev, device_id_type=MESH)

    for d in STEPS:
        hello(zdev(-d))
    for j in range(1, 4):
        for kk in range(2):
            hello(device(lax.rem(x + j, 4), y, z, kk))
            hello(device(x, lax.rem(y + j, 4), z, kk))
    hello(sib)

    @pl.when(jnp.logical_not(on_diagonal))
    def _():
        hello(turned(0))

    here[0].wait()

    p0 = pattern_ref[0, 0].astype(f32)
    p1 = pattern_ref[0, 1].astype(f32)
    vp[y, 0:T] = panel[:, 0:T] * p0 + panel[:, T:] * p1
    vp[y, T:H] = jnp.zeros((8, T), f32) + p1
    pl.semaphore_wait(bar, len(STEPS) + 14 - on_diagonal.astype(jnp.int32))

    sends = []

    def send(src, dst, ss, rs, dev, start=True):
        c = pltpu.make_async_remote_copy(
            src_ref=src, dst_ref=dst, send_sem=ss, recv_sem=rs,
            device_id=dev, device_id_type=MESH,
        )
        if start:
            c.start()
            sends.append((None, c))
        return c

    def drain():
        for me, c in sends:
            if me is None:
                c.wait_send()
            else:
                pl.when(jnp.logical_not(me))(c.wait_send)
        sends.clear()

    def send_or_keep(me, src, dst, ss, rs, dev):
        c = send(src, dst, ss, rs, dev, start=False)

        @pl.when(me)
        def _():
            pltpu.make_async_copy(src, dst, rs).start()

        @pl.when(jnp.logical_not(me))
        def _():
            c.start()

        sends.append((me, c))

    def halves(ref):
        v, s = ref[0:T], ref[T : T + 1]
        v1 = v * s
        return v - v1, v1

    v = vp.at[y]
    for n, piece in enumerate(PIECES):
        ds = pl.ds(*piece)
        send_or_keep(
            on_diagonal, vp.at[y, ds], vz.at[z, ds], ss_t.at[n], rs_z.at[n, z], turned(0)
        )
    for j in (2, 1, 3):
        send(v, v, ss_p.at[j - 1], rs_p.at[y], device(x, lax.rem(y + j, 4), z, k))

    def half(i, h):
        return abuf.at[i, pl.ds(h * 64, 64)]

    def send_a():
        i = lax.rem(y, 2) * 2 + k
        for h in (0, 1):
            for j, h in ((1, h), (3, 1 - h), (0, h)):
                src = a_ref.at[pl.ds(h * 64, 64)]
                dev = device(x, lax.rem(y + j, 4), z, ky)
                if j == 0:
                    send_or_keep(k == ky, src, half(i, h), ss_a.at[j, h], rs_a.at[i, h], dev)
                else:
                    send(src, half(i, h), ss_a.at[j, h], rs_a.at[i, h], dev)

    def hand_on_a():
        for r in range(2):
            d = lax.rem(y - 2 * k - r + 4, 4)
            h = jnp.where(d == 1, 0, 1)
            dev = device(x, jnp.where(d == 1, lax.rem(y + 1, 4), lax.rem(y + 3, 4)), z, k)
            for kk in range(2):
                i = r * 2 + kk
                c = send(half(i, h), half(i, h), ss_h.at[i], rs_a.at[i, h], dev, start=False)

                @pl.when(lax.rem(d, 2) == 1)
                def _():
                    arrived(half(i, h), rs_a.at[i, h])
                    c.start()

                sends.append((lax.rem(d, 2) == 0, c))

    def expand(ref, rel, zs):
        rows = pl.ds(pl.multiple_of(zs * T, T), T)
        for q, part in enumerate(halves(ref)):
            hi, lo = split(part)
            vhi[rel, rows, q * T : (q + 1) * T] = hi
            vlo[rel, rows, q * T : (q + 1) * T] = lo

    def pass_on(o, to, n):
        zs = zat(-o)
        part = vz.at[zs, pl.ds(*PIECES[n])]
        arrived(part, rs_z.at[n, zs])
        for c in to:
            send(part, part, ss_z.at[n, c + 7], rs_z.at[n, zs], zdev(c - o))

    def use(o):
        zs = zat(-o)
        tile = vz.at[zs]
        send(tile, vs.at[zs], ss_sib.at[zs], rs_sib.at[zs], sib)
        if o == -5:
            hand_on_a()
        if o == 0:
            send_a()
            for j in (2, 1, 3, 0):
                i = lax.rem(x, 2) * 2 + jnp.where(k == kx, 0, 1)
                dev = device(lax.rem(x + j, 4), y, z, kx)
                src = vz.at[z, pl.ds(T, 8)]
                if j == 0:
                    send_or_keep(k == kx, src, sy.at[i], ss_sy.at[j], rs_sy.at[i], dev)
                else:
                    send(src, sy.at[i], ss_sy.at[j], rs_sy.at[i], dev)
        expand(tile, 0, zs)

    for first, last in GROUPS:
        for n in range(len(PIECES)):
            for o, to in TREE[first:last]:
                pass_on(o, to, n)
        for o, _ in TREE[first:last]:
            use(o)

    for j in range(1, 4):
        i = lax.rem(y + j, 4)
        arrived(vp.at[i], rs_p.at[i])
    send(vp, vq, ss_q, rs_q, sib)
    arrived(vq, rs_q)
    for ref, kk in ((vp, k), (vq, 1 - k)):
        for ya in range(4):
            for q, part in enumerate(halves(ref.at[ya])):
                hi, lo = split(part.T)
                thi[kk * 2 + q, :, ya * T : (ya + 1) * T] = hi
                tlo[kk * 2 + q, :, ya * T : (ya + 1) * T] = lo

    for r in range(2):
        for kk in range(2):
            i = r * 2 + kk
            d = lax.rem(y - 2 * k - r + 4, 4)
            h = jnp.where(d == 1, 0, 1)

            @pl.when(lax.rem(d, 2) == 0)
            def _():
                arrived(half(i, h), rs_a.at[i, h])

            arrived(half(i, 1 - h), rs_a.at[i, 1 - h])
            hi, lo = split(abuf[i])
            ahi[r * T : (r + 1) * T, kk * 1024 : (kk + 1) * 1024] = hi
            alo[r * T : (r + 1) * T, kk * 1024 : (kk + 1) * 1024] = lo

    for o, _ in TREE:
        zs = zat(-o)
        arrived(vs.at[zs], rs_sib.at[zs])
        expand(vs.at[zs], 1, zs)
    for i in range(4):
        arrived(sy.at[i], rs_sy.at[i])

    for rel in range(2):
        acc = dot3(ahi[...], alo[...], vhi[rel], vlo[rel])
        for r in range(2):
            i = r * 2 + rel
            s = sy[i, 0:1]
            rows = acc[r * T : (r + 1) * T]
            op[i] = jnp.where(s > 0.5, rows[:, T:], rows[:, :T])
        for h in range(2):
            ds = pl.ds(h * 64, 64)
            for r in range(2):
                i = r * 2 + rel
                src, dst = op.at[i, ds], ob.at[x, ds]
                sems = ss_o.at[h, i], rs_o.at[h, x]
                if rel == 0:
                    send_or_keep(2 * k + r == x, src, dst, *sems, device(2 * k + r, y, z, k))
                else:
                    send(src, dst, *sems, device(2 * k + r, y, z, 1 - k))
    osend[T:H] = vz[z, T:H]
    for h, piece in enumerate(PIECES):
        lo = slice(h * 64, h * 64 + 64)
        for i in range(4):
            arrived(ob.at[i, pl.ds(h * 64, 64)], rs_o.at[h, i])
        osend[lo] = -((ob[0, lo] + ob[1, lo]) + (ob[2, lo] + ob[3, lo]))
        for j in (2, 1, 3):
            dev = device(lax.rem(x + j, 4), y, z, k)
            ds = pl.ds(*piece)
            send(osend.at[ds], oy.at[x, ds], ss_oy.at[h, j - 1], rs_oy.at[h, x], dev)
    send_or_keep(on_diagonal, osend.at[pl.ds(0, T)], ohome, ss_oh, rs_oh, turned(0))

    drain()

    def place(ref, ya):
        rows = pl.ds(pl.multiple_of(ya * T, T), T)
        for q, part in enumerate(halves(ref)):
            hi, lo = split(part)
            ohi[rows, q * T : (q + 1) * T] = hi
            olo[rows, q * T : (q + 1) * T] = lo

    place(osend, x)
    for j in (1, 3, 2):
        xa = lax.rem(x + j, 4)
        for h, piece in enumerate(PIECES):
            arrived(oy.at[xa, pl.ds(*piece)], rs_oy.at[h, xa])
        place(oy.at[xa], xa)

    zl, zb = lax.rem(z, 4), z // 4
    for j in (2, 1, 3, 0):
        b = lax.rem(zb + j, 4)
        u = dot3(thi[b], tlo[b], ohi[...], olo[...])
        for i in range(4):
            ubuf[i, b] = u[i * 32 : (i + 1) * 32]
        for i, d in enumerate(NEAR):
            src = ubuf.at[lax.rem(zl + way * d + 4, 4), b]
            send(src, un.at[i, b], ss_un.at[i, j], rs_un.at[i, b], zdev(d))
    drain()
    arrived(ohome, rs_oh)
    off_ref[...] = ohome[...]
    for j in (2, 1, 3, 0):
        b = lax.rem(zb + j, 4)
        for i in range(3):
            arrived(un.at[i, b], rs_un.at[i, b])
        ured[b] = (ubuf[zl, b] + un[0, b]) + (un[1, b] + un[2, b])
        dev = device(y, x, lax.rem(z + 4 * j, 16), k)
        if j:
            send(ured.at[b], uf.at[j], ss_uf.at[j], rs_uf.at[j], dev)
        else:
            send_or_keep(on_diagonal, ured.at[b], uf.at[j], ss_uf.at[j], rs_uf.at[j], dev)
    here[1].wait()
    total = diag[...]
    for j in (0, 1, 3, 2):
        arrived(uf.at[j], rs_uf.at[j])
        total = total - uf[j]
    out_ref[...] = total

    drain()


def place_results(o_ref, diag_ref, pattern_ref, off_out, diag_out):
    off_out[:, 0:T] = o_ref[...] * pattern_ref[0, 0].astype(f32)
    off_out[:, T:] = o_ref[...] * pattern_ref[0, 1].astype(f32)
    diag_out[...] = diag_ref[...]


def local(root_inverse, panel, pattern, diag_inverse):
    vmem, dma = pltpu.VMEM, pltpu.SemaphoreType.DMA
    parts = pl.pallas_call(
        kernel,
        out_shape=(
            jax.ShapeDtypeStruct((T, T), f32),
            jax.ShapeDtypeStruct(diag_inverse.shape, f32),
        ),
        in_specs=[
            pl.BlockSpec(memory_space=pl.ANY),
            pl.BlockSpec(memory_space=pl.ANY),
            pl.BlockSpec(memory_space=pltpu.SMEM),
            pl.BlockSpec(memory_space=pl.ANY),
        ],
        out_specs=(pl.BlockSpec(memory_space=pltpu.VMEM), pl.BlockSpec(memory_space=pltpu.VMEM)),
        scratch_shapes=[
            vmem((T, 2 * T), f32),
            vmem((32, 2 * T), f32),
            vmem((4, T, 1024), f32),
            vmem((16, H, T), f32),
            vmem((16, H, T), f32),
            vmem((4, H, T), f32),
            vmem((4, H, T), f32),
            vmem((4, 8, T), f32),
            vmem((4, T, T), f32),
            vmem((4, T, T), f32),
            vmem((H, T), f32),
            vmem((T, T), f32),
            vmem((4, H, T), f32),
            vmem((2 * T, 2048), bf16),
            vmem((2 * T, 2048), bf16),
            vmem((2, 2048, 2 * T), bf16),
            vmem((2, 2048, 2 * T), bf16),
            vmem((4, T, 4 * T), bf16),
            vmem((4, T, 4 * T), bf16),
            vmem((4 * T, 2 * T), bf16),
            vmem((4 * T, 2 * T), bf16),
            vmem((4, 4, 32, 2 * T), f32),
            vmem((3, 4, 32, 2 * T), f32),
            vmem((4, 32, 2 * T), f32),
            vmem((4, 32, 2 * T), f32),
            dma((2,)),
            dma((4, 2)), dma((4,)), dma((4, 2)),
            dma((2,)), dma((3,)), dma((4,)),
            dma((2, 16)), dma((2, 16)),
            dma((16,)), dma((16,)),
            dma((4,)), dma((4,)),
            dma, dma,
            dma((2, 4)), dma((2, 4)),
            dma, dma,
            dma((2, 3)), dma((2, 4)),
            dma((3, 4)), dma((3, 4)),
            dma((4,)), dma((4,)),
        ],
        compiler_params=pltpu.CompilerParams(
            collective_id=0, has_side_effects=True, vmem_limit_bytes=56 << 20
        ),
    )(root_inverse, panel, pattern, diag_inverse)
    return pl.pallas_call(
        place_results,
        out_shape=tuple(jax.ShapeDtypeStruct(p.shape, f32) for p in (panel, diag_inverse)),
        in_specs=[
            pl.BlockSpec(memory_space=pltpu.VMEM),
            pl.BlockSpec(memory_space=pltpu.VMEM),
            pl.BlockSpec(memory_space=pltpu.SMEM),
        ],
        out_specs=(pl.BlockSpec(memory_space=pltpu.VMEM), pl.BlockSpec(memory_space=pltpu.VMEM)),
    )(*parts, pattern)


def solution(mesh):
    spec = P(("sub", "row"), "col")
    return jax.shard_map(
        local, mesh=mesh, in_specs=(spec,) * 4, out_specs=(spec,) * 2, check_vma=False
    )
```
